1024 devices in a mesh: section: 8 (over x_lo, core), expert: 16 (over z, x_hi), dp: 8 (over y).
Axes of the slice: x: 8 (x_hi: 2, x_lo: 4; x = x_hi * 4 + x_lo), y: 8, z: 8, core: 2. Of those that a mesh axis runs over, the one named last changes fastest.
Arguments:
- falling_grad: bfloat16 [8, 1024, 7168], P('section', 'expert', 'dp'), may hold values from -6 to 6
- rising_grad: bfloat16 [8, 1024, 7168], P('section', 'expert', 'dp'), may hold values from -6 to 6
- routes_falling: int32 [8, 1024, 8], P('section', 'expert'), may hold values from 0 to 15, all different within a row; in each aligned block of 64 rows (0 to 63, 64 to 127, ..., all dimensions but the last counted through in order) at most 40 rows name the same one
- routes_rising: int32 [8, 1024, 8], P('section', 'expert'), may hold values from 0 to 15, all different within a row; in each aligned block of 64 rows (0 to 63, 64 to 127, ..., all dimensions but the last counted through in order) at most 40 rows name the same one
- scores_falling: float32 [8, 1024, 8], P('section', 'expert'), may hold values from 0.05 to 0.95
- scores_rising: float32 [8, 1024, 8], P('section', 'expert'), may hold values from 0.05 to 0.95
- down_weight: bfloat16 [8, 16, 1024, 7168], P('section', 'expert', None, 'dp'), may hold values from -0.1875 to 0.1875
- saved_falling: bfloat16 [8, 1024, 16, 640], P('section', 'dp', 'expert'), may hold values from -0.29882812 to 0.29882812
- saved_rising: bfloat16 [8, 1024, 16, 640], P('section', 'dp', 'expert'), may hold values from -0.29882812 to 0.29882812
Outputs:
- hidden_falling: bfloat16 [8, 1024, 16, 640], P('section', 'dp', 'expert')
- hidden_rising: bfloat16 [8, 1024, 16, 640], P('section', 'dp', 'expert')
- logits_falling: float32 [8, 1024, 8], P('section', 'expert')
- logits_rising: float32 [8, 1024, 8], P('section', 'expert')
The draws below stay inside these ranges and needn't reach their ends.
Inputs may be any that keep to these rules, and one draw needn't show every extreme that they name: `routes_falling`: A token names 8 different experts; in each aligned block of 64 tokens (the tokens of one section and one index of expert) no expert is named by more than 40 tokens, and in some blocks one expert by exactly 40. `routes_rising`: A token names 8 different experts; in each aligned block of 64 tokens (the tokens of one section and one index of expert) no expert is named by more than 40 tokens, and in some blocks one expert by exactly 40.
All inputs are finite; a program needn't handle non-finite values.
Results may differ from the reference program's by a relative error of at most 0.019.
Values may be sent and summed in bfloat16 or wider, within the bound.
No kernel may reach another device: no remote copies, remote signals or barrier semaphores. Data moves between devices by JAX's collectives and lax.ppermute only.
A program may use at most 32 MiB of HBM per device.

```python
import math
import jax
import jax.numpy as jnp
import numpy as np
from jax import lax

D = 7168
TOPK = 8
FF = 1024
EXPERTS = 16
TOK_DEV = 64
SECTIONS = 8
TOKENS = 1024
CAP = 40
SLOTS = 640
N_EXPERT = 16
N_DP = 8


def block_scale(own_key, shape, cuts, smallest, high):
    gain = 1.0
    for dim, shards_of in cuts:
        heights = jax.random.uniform(jax.random.fold_in(jax.random.fold_in(own_key, 6), dim), (shards_of,), jnp.float32, smallest / len(cuts), high / len(cuts))
        gain = gain * jnp.repeat(jnp.exp(heights), shape[dim] // shards_of).reshape((-1,) + (1,) * (len(shape) - 1 - dim))
    return gain


def routed_block(key, own, number, rows, count, top, bound, lean):
    sequence = jax.random.permutation(key, count)
    crowded, usual = shares(count, rows * top, bound, lean, True), shares(count, rows * top, bound, lean, False)
    places = jnp.arange(count)

    def named(lengths, rotation):
        used = int((lengths > 0).sum())
        fixed = max(1, used // 4)
        shifted = fixed + (places - fixed + rotation * (used - fixed)) % max(1, count - fixed)
        return jnp.zeros((count,), jnp.int32).at[sequence[jnp.where(places < fixed, places, shifted)]].set(jnp.asarray(lengths, jnp.int32))

    lengths = jnp.where(number % 4 == 0, named(crowded, number // 4), named(usual, number - number // 4 - 1))
    mixed = jax.random.permutation(jax.random.fold_in(own, 3), count)
    source_of, receiver = mixed[0:count // 2 * 2:2], mixed[1:count // 2 * 2:2]
    slack = jnp.minimum(lengths[source_of] - 1, bound - lengths[receiver]) // 2
    slack = jnp.where((source_of == sequence[0]) | (receiver == sequence[0]) | (lengths[receiver] == 0), 0, jnp.maximum(slack, 0))
    shifted = jax.random.randint(jax.random.fold_in(own, 4), (count // 2,), 0, 1 << 20) % (slack + 1)
    lengths = lengths.at[source_of].add(-shifted).at[receiver].add(shifted)
    labels = jnp.searchsorted(jnp.cumsum(lengths), jnp.arange(rows * top), side="right").astype(jnp.int32)
    listing = labels.reshape(top, rows).T
    listing = listing[jax.random.permutation(jax.random.fold_in(own, 1), rows)]
    rotation = jax.random.randint(jax.random.fold_in(own, 2), (rows, 1), 0, top)
    return jnp.take_along_axis(listing, (jnp.arange(top)[None, :] + rotation) % top, axis=1)


def shares(count, total, limit, skew, full):
    weights = [(1 << 20) // math.isqrt(grade ** skew) + 1 for grade in range(1, count + 1)]
    largest = limit if full else min(limit, max(-(-total // count), total * weights[0] // sum(weights)))
    least = 1 if total - largest >= count - 1 else 0
    counts, surplus = [largest] + [least] * (count - 1), total - largest - least * (count - 1)
    while surplus > 0:
        candidates = [i for i in range(1, count) if counts[i] < largest] or [i for i in range(1, count) if counts[i] < limit]
        mass, budget = sum([weights[i] for i in candidates]), surplus
        for i in candidates:
            extra = min(limit - counts[i], max(1, budget * weights[i] // mass), surplus)
            counts[i] = counts[i] + extra
            surplus = surplus - extra
    return np.array(counts)


def bell_draw(rng, extent, width, most, shards=(), kind=jnp.bfloat16):
    array = jax.random.normal(rng, extent, jnp.float32) * width
    if len(shards) > 0:
        array = block_scale(rng, extent, shards, -0.22, 0.18) * array
    return jnp.clip(array, min=-most, max=most).astype(kind)


def setup_inputs(seed: int = 0) -> dict:
    keys = jax.random.split(jax.random.key(seed), 10)
    falling_grad = bell_draw(keys[0], (SECTIONS, TOKENS, D), 1.0, 6.0, ((0, 8), (1, 16), (2, 8)))
    rising_grad = bell_draw(keys[1], (SECTIONS, TOKENS, D), 1.0, 6.0, ((0, 8), (1, 16), (2, 8)))
    routes_falling_keys = jax.random.split(jax.random.fold_in(keys[2], 1), SECTIONS * TOKENS // TOK_DEV)
    routes_falling_turns = jax.random.permutation(jax.random.fold_in(keys[2], 3), SECTIONS * TOKENS // TOK_DEV)
    routes_falling = jax.vmap(lambda own, number: routed_block(jax.random.fold_in(keys[2], 2), own, number, TOK_DEV, EXPERTS, TOPK, CAP, 2))(routes_falling_keys, routes_falling_turns).reshape((SECTIONS, TOKENS, TOPK))
    routes_rising_keys = jax.random.split(jax.random.fold_in(keys[3], 1), SECTIONS * TOKENS // TOK_DEV)
    routes_rising_turns = jax.random.permutation(jax.random.fold_in(keys[3], 3), SECTIONS * TOKENS // TOK_DEV)
    routes_rising = jax.vmap(lambda own, number: routed_block(jax.random.fold_in(keys[3], 2), own, number, TOK_DEV, EXPERTS, TOPK, CAP, 2))(routes_rising_keys, routes_rising_turns).reshape((SECTIONS, TOKENS, TOPK))
    scores_falling = jnp.clip(0.05 + 0.9 * jax.random.uniform(keys[4], (SECTIONS, TOKENS, TOPK), jnp.float32) ** block_scale(keys[4], (SECTIONS, TOKENS, TOPK), ((0, 8), (1, 16)), -0.2, 0.2), 0.05, 0.95)
    scores_rising = jnp.clip(0.05 + 0.9 * jax.random.uniform(keys[5], (SECTIONS, TOKENS, TOPK), jnp.float32) ** block_scale(keys[5], (SECTIONS, TOKENS, TOPK), ((0, 8), (1, 16)), -0.2, 0.2), 0.05, 0.95)
    down_weight = bell_draw(keys[6], (SECTIONS, EXPERTS, FF, D), FF ** -0.5, 0.1875, ((0, 8), (1, 16), (3, 8)))
    saved_falling = bell_draw(keys[7], (SECTIONS, FF, EXPERTS, SLOTS), 0.05, 0.29882812, ((0, 8), (1, 8), (2, 16)))
    saved_rising = bell_draw(keys[8], (SECTIONS, FF, EXPERTS, SLOTS), 0.05, 0.29882812, ((0, 8), (1, 8), (2, 16)))
    return dict(falling_grad=falling_grad, rising_grad=rising_grad, routes_falling=routes_falling, routes_rising=routes_rising, scores_falling=scores_falling, scores_rising=scores_rising, down_weight=down_weight, saved_falling=saved_falling, saved_rising=saved_rising)


route_scale = 2.5


def block_places(block_ids):
    expert_hot = (block_ids[:, :, None] == jnp.arange(EXPERTS, dtype=jnp.int32)[None, None, :]).astype(jnp.int32)
    flat_hot = expert_hot.reshape(TOK_DEV * TOPK, EXPERTS)
    earlier = (jnp.cumsum(flat_hot, axis=0) - flat_hot).reshape(TOK_DEV, TOPK, EXPERTS)
    position = jnp.sum(earlier * expert_hot, axis=2)
    slot_hot = (position[:, :, None] == jnp.arange(CAP, dtype=jnp.int32)[None, None, :]).astype(jnp.int32)
    return (expert_hot[:, :, :, None] * slot_hot[:, :, None, :]).astype(jnp.float32)


def expert_pass(pieces):
    expert_rows, expert_weight, expert_gate, expert_saved = pieces
    group_rows = expert_rows.astype(jnp.float32).reshape(N_EXPERT * CAP, N_DP, D // N_DP)
    group_weight = expert_weight.astype(jnp.float32).reshape(FF, N_DP, D // N_DP)
    partial_sums = jnp.einsum("rgd,fgd->gfr", group_rows, group_weight, precision=lax.Precision.HIGHEST)
    partial_sums = lax.optimization_barrier(partial_sums.astype(jnp.bfloat16))
    hidden_terms = jnp.sum(partial_sums.astype(jnp.float32), axis=0)
    gate_row = expert_gate.reshape(1, N_EXPERT * CAP).astype(jnp.float32)
    hidden = (gate_row * hidden_terms).astype(jnp.bfloat16)
    slot_grad = jnp.sum(hidden_terms * expert_saved.astype(jnp.float32), axis=0)
    return hidden, slot_grad


def one_section(pieces):
    arriving, section_ids, section_scores, section_weight, section_saved = pieces
    token_blocks = arriving.astype(jnp.float32).reshape(N_EXPERT, TOK_DEV, D)
    placed = jax.vmap(block_places)(section_ids.reshape(N_EXPERT, TOK_DEV, TOPK))
    score_blocks = section_scores.reshape(N_EXPERT, TOK_DEV, TOPK)
    score_total = jnp.sum(score_blocks, axis=2, keepdims=True)
    gate_values = route_scale * score_blocks / score_total
    token_place = jnp.sum(placed, axis=2)
    rows = jnp.einsum("jtec,jtd->ejcd", token_place, token_blocks, precision=lax.Precision.HIGHEST).astype(jnp.bfloat16)
    slot_gate = jnp.einsum("jtkec,jtk->ejc", placed, gate_values, precision=lax.Precision.HIGHEST).astype(jnp.bfloat16)
    hidden, slot_grad = lax.map(expert_pass, (rows, section_weight, slot_gate, jnp.moveaxis(section_saved, 1, 0)))
    slot_back = jnp.transpose(slot_grad.reshape(EXPERTS, N_EXPERT, CAP), (1, 0, 2))
    route_grad = jnp.sum(placed * slot_back[:, None, None, :, :], axis=(3, 4))
    weighted_mean = jnp.sum(route_grad * score_blocks, axis=2, keepdims=True) / score_total
    logit_grad = route_scale / score_total * (route_grad - weighted_mean) * score_blocks * (1.0 - score_blocks)
    return jnp.moveaxis(hidden, 0, 1), logit_grad.reshape(TOKENS, TOPK)


def reference(falling_grad, rising_grad, routes_falling, routes_rising, scores_falling, scores_rising, down_weight, saved_falling, saved_rising):
    arriving_falling = jnp.roll(falling_grad, -1, axis=0)
    arriving_rising = jnp.roll(rising_grad, 1, axis=0)
    hidden_falling, logits_falling = lax.map(one_section, (arriving_falling, routes_falling, scores_falling, down_weight, saved_falling))
    hidden_rising, logits_rising = lax.map(one_section, (arriving_rising, routes_rising, scores_rising, down_weight, saved_rising))
    return (hidden_falling, hidden_rising, logits_falling, logits_rising)
```

```python
import functools

import jax
import jax.numpy as jnp
from jax import lax
from jax.experimental import pallas as pl
from jax.experimental.pallas import tpu as pltpu
from jax.sharding import PartitionSpec as P

route_scale = 2.5
META = 8
NT = (((1,), (1,)), ((), ()))
f32 = jnp.float32
bf16 = jnp.bfloat16


def pack_kernel(rf, sf, rr, sr, out, buf):
    top, tok = rf.shape
    buf[...] = jnp.zeros_like(buf)
    for m, (routes, scores) in enumerate(((rf, sf), (rr, sr))):
        ids = routes[...].astype(f32)
        s = scores[...]
        gate = route_scale * s / jnp.sum(s, axis=0, keepdims=True)
        for k in range(top):
            buf[2 * m : 2 * m + 1, k * tok : (k + 1) * tok] = ids[k : k + 1]
            buf[2 * m + 1 : 2 * m + 2, k * tok : (k + 1) * tok] = gate[k : k + 1]
    out[...] = buf[...].astype(out.dtype)


def expert_kernel(blocks, tok, top, cap, info, *refs):
    msgs = refs[:blocks]
    w_ref, saved_ref, part_ref, slot_ref, gate_ref = refs[blocks : blocks + 5]
    rows, rows16, gcol, meta = refs[blocks + 5 :]
    slots = blocks * cap
    lanes = 2 * tok

    @pl.when(pl.program_id(0) == 0)
    def _():
        slot_ref[...] = jnp.zeros_like(slot_ref)
        for b in range(blocks):
            meta[b * META : (b + 1) * META, :] = msgs[b][lanes : lanes + META, : top * tok].astype(f32)
        vals = meta[...]
        mine = (vals == info[0].astype(f32)).astype(f32)
        t_in = lax.rem(lax.broadcasted_iota(jnp.int32, (top * tok, lanes), 0), tok)
        t_out = lax.rem(lax.broadcasted_iota(jnp.int32, (top * tok, lanes), 1), tok)
        same = (t_in == t_out).astype(f32).astype(bf16)
        before = (t_in < t_out).astype(f32).astype(bf16)
        hot = mine.astype(bf16)
        named = jnp.dot(hot, same, preferred_element_type=f32)
        place = jnp.dot(hot, before, preferred_element_type=f32)
        picked = (pltpu.roll(mine, 1, 0) * vals).astype(bf16)
        gates = jnp.dot(picked, same, preferred_element_type=f32)
        rising = lax.broadcasted_iota(jnp.int32, (1, lanes), 1) >= tok
        shift = jnp.where(rising, float(cap), 0.0)
        slot_id = lax.broadcasted_iota(jnp.int32, (2 * cap, lanes), 0).astype(f32)
        for b in range(blocks):
            r = b * META
            name = jnp.where(rising, named[r + 2 : r + 3], named[r : r + 1])
            pos = jnp.where(rising, place[r + 2 : r + 3], place[r : r + 1])
            gate = jnp.where(rising, gates[r + 3 : r + 4], gates[r + 1 : r + 2])
            target = jnp.where(name > 0.5, pos + shift, -1.0)
            put = (slot_id == target).astype(f32)
            got = jnp.dot(put.astype(bf16), msgs[b][:lanes, :], preferred_element_type=f32)
            col = jnp.broadcast_to(jnp.sum(put * gate, axis=1, keepdims=True), (2 * cap, gcol.shape[2]))
            at = pl.ds(pl.multiple_of(info[1 + b] * cap, 8), cap)
            for m in range(2):
                rows[m, at, :] = got[m * cap : (m + 1) * cap]
                gcol[m, at, :] = col[m * cap : (m + 1) * cap]
        first = (lax.broadcasted_iota(jnp.int32, (8, gcol.shape[2]), 1) == 0).astype(f32).astype(bf16)
        for m in range(2):
            rows16[m] = rows[m].astype(bf16)
            gate_ref[:, m * slots : (m + 1) * slots] = lax.dot_general(
                first, gcol[m].astype(bf16), NT, preferred_element_type=f32
            )

    w = w_ref[...]
    for m in range(2):
        cols = slice(m * slots, (m + 1) * slots)
        part = lax.dot_general(w, rows16[m], NT, preferred_element_type=f32).astype(bf16)
        part_ref[:, cols] = part
        prod = part.astype(f32) * saved_ref[:, cols].astype(f32)
        slot_ref[:, cols] += jnp.sum(prod.reshape(-1, 8, slots), axis=0)


def logits_kernel(cap, rf, sf, rr, sr, back, out_f, out_r, grad):
    top, tok = rf.shape
    experts = back.shape[0]
    ids = lax.broadcasted_iota(jnp.int32, (experts, tok), 0)
    t0 = lax.broadcasted_iota(jnp.int32, (tok, tok), 0)
    t1 = lax.broadcasted_iota(jnp.int32, (tok, tok), 1)
    before = (t0 < t1).astype(f32).astype(bf16)
    for m, (routes, scores, out) in enumerate(((rf, sf, out_f), (rr, sr, out_r))):
        named = jnp.zeros((experts, tok), f32)
        for k in range(top):
            named += (routes[k : k + 1, :] == ids).astype(f32)
        place = jnp.dot(named.astype(bf16), before, preferred_element_type=f32)
        vals = jnp.zeros((experts, tok), f32)
        for c in range(cap):
            vals += jnp.where(place == float(c), back[:, m * cap + c : m * cap + c + 1], 0.0)
        for k in range(top):
            chosen = jnp.where(routes[k : k + 1, :] == ids, vals, 0.0)
            grad[k : k + 1, :] = jnp.sum(chosen, axis=0, keepdims=True)
        s = scores[...]
        total = jnp.sum(s, axis=0, keepdims=True)
        mean = jnp.sum(grad[...] * s, axis=0, keepdims=True) / total
        out[...] = route_scale / total * (grad[...] - mean) * s * (1.0 - s)


def shards(
    falling_grad,
    rising_grad,
    routes_falling,
    routes_rising,
    scores_falling,
    scores_rising,
    down_weight,
    saved_falling,
    saved_rising,
):
    blocks = lax.axis_size("expert")
    sections = lax.axis_size("section")
    dp = lax.axis_size("dp")
    tok, width = falling_grad.shape[1:]
    top = routes_falling.shape[2]
    ff_shard, slots = saved_falling.shape[1], saved_falling.shape[3]
    cap = slots // blocks
    ff = ff_shard * dp
    depth = blocks // 2
    lanes = 2 * tok

    side = (
        routes_falling[0].T,
        scores_falling[0].T,
        routes_rising[0].T,
        scores_rising[0].T,
    )
    saved = jnp.concatenate(
        [saved_falling.reshape(ff_shard, slots), saved_rising.reshape(ff_shard, slots)], axis=1
    )
    saved_all = lax.all_gather(saved, "dp", tiled=True)

    def hop(array, by, flip):
        pairs = [
            (s * blocks + e, (s + by) % sections * blocks + (e ^ flip))
            for s in range(sections)
            for e in range(blocks)
        ]
        return lax.ppermute(array, ("section", "expert"), pairs)

    own_f, own_r = hop(falling_grad[0], -1, 0), hop(rising_grad[0], 1, 0)
    far_f, far_r = hop(falling_grad[0], -1, 1), hop(rising_grad[0], 1, 1)
    meta = pl.pallas_call(
        pack_kernel,
        out_shape=jax.ShapeDtypeStruct((META, width), bf16),
        scratch_shapes=[pltpu.VMEM((META, width), f32)],
    )(*side)
    far_meta = hop(meta, 0, 1)
    own = jnp.concatenate([own_f, own_r, meta], axis=0)
    far = jnp.concatenate([far_f, far_r, far_meta], axis=0)

    up = [(i, (i + 2) % blocks) for i in range(blocks)]
    down = [(i, (i - 2) % blocks) for i in range(blocks)]
    me = lax.axis_index("expert")
    level, column = me // 2, me % 2
    msgs, index = [own, far], [me, level * 2 + 1 - column]
    own_up = own_down = own
    far_up = far_down = far
    for t in range(1, depth // 2 + 1):
        own_up = lax.ppermute(own_up, "expert", up)
        msgs.append(own_up)
        index.append((level - t) % depth * 2 + column)
        if t < depth // 2:
            own_down = lax.ppermute(own_down, "expert", down)
            msgs.append(own_down)
            index.append((level + t) % depth * 2 + column)
            far_up = lax.ppermute(far_up, "expert", up)
            msgs.append(far_up)
            index.append((level - t) % depth * 2 + 1 - column)
        far_down = lax.ppermute(far_down, "expert", down)
        msgs.append(far_down)
        index.append((level + t) % depth * 2 + 1 - column)
    info = jnp.stack([me] + index).astype(jnp.int32)

    tile = min(256, ff)
    whole = pl.BlockSpec((lanes + META, width), lambda i: (0, 0))
    partial, slot_part, gates = pl.pallas_call(
        functools.partial(expert_kernel, blocks, tok, top, cap),
        grid=(ff // tile,),
        in_specs=[pl.BlockSpec(memory_space=pltpu.SMEM)]
        + [whole] * blocks
        + [
            pl.BlockSpec((tile, width), lambda i: (i, 0)),
            pl.BlockSpec((tile, 2 * slots), lambda i: (i, 0)),
        ],
        out_specs=[
            pl.BlockSpec((tile, 2 * slots), lambda i: (i, 0)),
            pl.BlockSpec((8, 2 * slots), lambda i: (0, 0)),
            pl.BlockSpec((8, 2 * slots), lambda i: (0, 0)),
        ],
        out_shape=[
            jax.ShapeDtypeStruct((ff, 2 * slots), bf16),
            jax.ShapeDtypeStruct((8, 2 * slots), f32),
            jax.ShapeDtypeStruct((8, 2 * slots), f32),
        ],
        scratch_shapes=[
            pltpu.VMEM((2, slots, width), f32),
            pltpu.VMEM((2, slots, width), bf16),
            pltpu.VMEM((2, slots, 128), f32),
            pltpu.VMEM((blocks * META, top * tok), f32),
        ],
        compiler_params=pltpu.CompilerParams(vmem_limit_bytes=40 * 1024 * 1024),
        cost_estimate=pl.CostEstimate(
            flops=4 * ff * width * slots, bytes_accessed=16 * 1024 * 1024, transcendentals=0
        ),
    )(info, *msgs, down_weight.reshape(ff, width), saved_all)

    terms = lax.psum_scatter(partial, "dp", scatter_dimension=0, tiled=True)
    slot_grad = lax.psum(jnp.sum(slot_part, axis=0), "dp")
    home = jnp.transpose(slot_grad.reshape(2, blocks, cap), (1, 0, 2)).reshape(blocks, 2 * cap)
    back = lax.all_to_all(home, "expert", split_axis=0, concat_axis=0, tiled=True)
    logits = pl.pallas_call(
        functools.partial(logits_kernel, cap),
        out_shape=[jax.ShapeDtypeStruct((top, tok), f32)] * 2,
        scratch_shapes=[pltpu.VMEM((top, tok), f32)],
    )(*side, back)
    scaled = (gates[:1] * terms.astype(f32)).astype(bf16)
    hidden = [scaled[:, m * slots : (m + 1) * slots].reshape(1, ff_shard, 1, slots) for m in range(2)]
    return (*hidden, *(g.T[None] for g in logits))


def solution(mesh):
    in_specs = (
        P("section", "expert", "dp"),
        P("section", "expert", "dp"),
        P("section", "expert", None),
        P("section", "expert", None),
        P("section", "expert", None),
        P("section", "expert", None),
        P("section", "expert", None, "dp"),
        P("section", "dp", "expert", None),
        P("section", "dp", "expert", None),
    )
    out_specs = (
        P("section", "dp", "expert", None),
        P("section", "dp", "expert", None),
        P("section", "expert", None),
        P("section", "expert", None),
    )
    return jax.shard_map(shards, mesh=mesh, in_specs=in_specs, out_specs=out_specs, check_vma=False)
```

```python
import functools

import jax
import jax.numpy as jnp
from jax import lax
from jax.experimental import pallas as pl
from jax.experimental.pallas import tpu as pltpu
from jax.sharding import PartitionSpec as P

route_scale = 2.5
META = 8
NT = (((1,), (1,)), ((), ()))
f32 = jnp.float32
bf16 = jnp.bfloat16


def pack_kernel(rf, sf, rr, sr, out, buf):
    top, tok = rf.shape
    buf[...] = jnp.zeros_like(buf)
    for m, (routes, scores) in enumerate(((rf, sf), (rr, sr))):
        ids = routes[...].astype(f32)
        s = scores[...]
        gate = route_scale * s / jnp.sum(s, axis=0, keepdims=True)
        for k in range(top):
            buf[2 * m : 2 * m + 1, k * tok : (k + 1) * tok] = ids[k : k + 1]
            buf[2 * m + 1 : 2 * m + 2, k * tok : (k + 1) * tok] = gate[k : k + 1]
    out[...] = buf[...].astype(out.dtype)


def expert_kernel(blocks, tok, top, cap, info, *refs):
    msgs = refs[:blocks]
    w_hbm, saved_hbm, part_hbm, slot_ref, gate_ref = refs[blocks : blocks + 5]
    rows, rows16, gcol, meta, w_ref, saved_ref, part_ref, w_sem, saved_sem, part_sem = refs[blocks + 5 :]
    slots = blocks * cap
    lanes = 2 * tok
    tiles = w_sem.shape[0]
    tile = w_ref.shape[0] // tiles
    parts = [pl.ds(i * tile, tile) for i in range(tiles)]
    fetched = []
    for i, at in enumerate(parts):
        pair = (
            pltpu.make_async_copy(w_hbm.at[at], w_ref.at[at], w_sem.at[i]),
            pltpu.make_async_copy(saved_hbm.at[at], saved_ref.at[at], saved_sem.at[i]),
        )
        for copy in pair:
            copy.start()
        fetched.append(pair)

    for b in range(blocks):
        meta[b * META : (b + 1) * META, :] = msgs[b][lanes : lanes + META, : top * tok].astype(f32)
    vals = meta[...]
    mine = (vals == info[0].astype(f32)).astype(f32)
    t_in = lax.rem(lax.broadcasted_iota(jnp.int32, (top * tok, lanes), 0), tok)
    t_out = lax.rem(lax.broadcasted_iota(jnp.int32, (top * tok, lanes), 1), tok)
    same = (t_in == t_out).astype(f32).astype(bf16)
    before = (t_in < t_out).astype(f32).astype(bf16)
    hot = mine.astype(bf16)
    named = jnp.dot(hot, same, preferred_element_type=f32)
    place = jnp.dot(hot, before, preferred_element_type=f32)
    picked = (pltpu.roll(mine, 1, 0) * vals).astype(bf16)
    gates = jnp.dot(picked, same, preferred_element_type=f32)
    rising = lax.broadcasted_iota(jnp.int32, (1, lanes), 1) >= tok
    shift = jnp.where(rising, float(cap), 0.0)
    slot_id = lax.broadcasted_iota(jnp.int32, (2 * cap, lanes), 0).astype(f32)
    for b in range(blocks):
        r = b * META
        name = jnp.where(rising, named[r + 2 : r + 3], named[r : r + 1])
        pos = jnp.where(rising, place[r + 2 : r + 3], place[r : r + 1])
        gate = jnp.where(rising, gates[r + 3 : r + 4], gates[r + 1 : r + 2])
        target = jnp.where(name > 0.5, pos + shift, -1.0)
        put = (slot_id == target).astype(f32)
        got = jnp.dot(put.astype(bf16), msgs[b][:lanes, :], preferred_element_type=f32)
        col = jnp.broadcast_to(jnp.sum(put * gate, axis=1, keepdims=True), (2 * cap, gcol.shape[2]))
        at = pl.ds(pl.multiple_of(info[1 + b] * cap, 8), cap)
        for m in range(2):
            rows[m, at, :] = got[m * cap : (m + 1) * cap]
            gcol[m, at, :] = col[m * cap : (m + 1) * cap]
    first = (lax.broadcasted_iota(jnp.int32, (8, gcol.shape[2]), 1) == 0).astype(f32).astype(bf16)
    for m in range(2):
        rows16[m] = rows[m].astype(bf16)
        gate_ref[:, m * slots : (m + 1) * slots] = lax.dot_general(
            first, gcol[m].astype(bf16), NT, preferred_element_type=f32
        )

    sent = []
    for i, at in enumerate(parts):
        for copy in fetched[i]:
            copy.wait()
        w = w_ref[at, :]
        for m in range(2):
            cols = slice(m * slots, (m + 1) * slots)
            part = lax.dot_general(w, rows16[m], NT, preferred_element_type=f32).astype(bf16)
            part_ref[at, cols] = part
            prod = part.astype(f32) * saved_ref[at, cols].astype(f32)
            total = jnp.sum(prod.reshape(-1, 8, slots), axis=0)
            slot_ref[:, cols] = total if i == 0 else slot_ref[:, cols] + total
        copy = pltpu.make_async_copy(part_ref.at[at], part_hbm.at[at], part_sem.at[i])
        copy.start()
        sent.append(copy)
    for copy in sent:
        copy.wait()


def logits_kernel(cap, rf, sf, rr, sr, back, out_f, out_r, grad):
    top, tok = rf.shape
    experts = back.shape[0]
    ids = lax.broadcasted_iota(jnp.int32, (experts, tok), 0)
    t0 = lax.broadcasted_iota(jnp.int32, (tok, tok), 0)
    t1 = lax.broadcasted_iota(jnp.int32, (tok, tok), 1)
    before = (t0 < t1).astype(f32).astype(bf16)
    for m, (routes, scores, out) in enumerate(((rf, sf, out_f), (rr, sr, out_r))):
        named = jnp.zeros((experts, tok), f32)
        for k in range(top):
            named += (routes[k : k + 1, :] == ids).astype(f32)
        place = jnp.dot(named.astype(bf16), before, preferred_element_type=f32)
        vals = jnp.zeros((experts, tok), f32)
        for c in range(cap):
            vals += jnp.where(place == float(c), back[:, m * cap + c : m * cap + c + 1], 0.0)
        for k in range(top):
            chosen = jnp.where(routes[k : k + 1, :] == ids, vals, 0.0)
            grad[k : k + 1, :] = jnp.sum(chosen, axis=0, keepdims=True)
        s = scores[...]
        total = jnp.sum(s, axis=0, keepdims=True)
        mean = jnp.sum(grad[...] * s, axis=0, keepdims=True) / total
        out[...] = route_scale / total * (grad[...] - mean) * s * (1.0 - s)


def shards(
    falling_grad,
    rising_grad,
    routes_falling,
    routes_rising,
    scores_falling,
    scores_rising,
    down_weight,
    saved_falling,
    saved_rising,
):
    blocks = lax.axis_size("expert")
    sections = lax.axis_size("section")
    dp = lax.axis_size("dp")
    tok, width = falling_grad.shape[1:]
    top = routes_falling.shape[2]
    ff_shard, slots = saved_falling.shape[1], saved_falling.shape[3]
    cap = slots // blocks
    ff = ff_shard * dp
    depth = blocks // 2
    lanes = 2 * tok

    side = (
        routes_falling[0].T,
        scores_falling[0].T,
        routes_rising[0].T,
        scores_rising[0].T,
    )
    def hop(array, by, flip):
        pairs = [
            (s * blocks + e, (s + by) % sections * blocks + (e ^ flip))
            for s in range(sections)
            for e in range(blocks)
        ]
        return lax.ppermute(array, ("section", "expert"), pairs)

    own_f, own_r = hop(falling_grad[0], -1, 0), hop(rising_grad[0], 1, 0)
    meta = pl.pallas_call(
        pack_kernel,
        out_shape=jax.ShapeDtypeStruct((META, width), bf16),
        scratch_shapes=[pltpu.VMEM((META, width), f32)],
    )(*side)
    own = jnp.concatenate([own_f, own_r, meta], axis=0)
    far = hop(own, 0, 1)

    saved = jnp.concatenate(
        [saved_falling.reshape(ff_shard, slots), saved_rising.reshape(ff_shard, slots)], axis=1
    )
    own_ring, saved = lax.optimization_barrier((own, saved))
    saved_all = lax.all_gather(saved, "dp", tiled=True)

    up = [(i, (i + 2) % blocks) for i in range(blocks)]
    down = [(i, (i - 2) % blocks) for i in range(blocks)]
    me = lax.axis_index("expert")
    level, column = me // 2, me % 2
    msgs, index = [own, far], [me, level * 2 + 1 - column]

    def step(rise, fall, side, t):
        if rise is not None:
            rise = lax.ppermute(rise, "expert", up)
            msgs.append(rise)
            index.append((level - t) % depth * 2 + side)
        if fall is not None:
            fall = lax.ppermute(fall, "expert", down)
            msgs.append(fall)
            index.append((level + t) % depth * 2 + side)
        return rise, fall

    half = depth // 2
    own_rise = own_fall = own_ring
    for t in range(1, half):
        own_rise, own_fall = step(own_rise, own_fall, column, t)
        if t == 1:
            own_rise, own_fall, far = lax.optimization_barrier((own_rise, own_fall, far))
            msgs[1:] = far, own_rise, own_fall
    step(own_rise, None, column, half)
    far_rise = far_fall = far
    for t in range(1, half):
        far_rise, far_fall = step(far_rise, far_fall, 1 - column, t)
    step(None, far_fall, 1 - column, half)
    info = jnp.stack([me] + index).astype(jnp.int32)

    tiles = max(1, ff // 256)
    vmem, hbm = pl.BlockSpec(memory_space=pltpu.VMEM), pl.BlockSpec(memory_space=pltpu.HBM)
    partial, slot_part, gates = pl.pallas_call(
        functools.partial(expert_kernel, blocks, tok, top, cap),
        in_specs=[pl.BlockSpec(memory_space=pltpu.SMEM)] + [vmem] * blocks + [hbm, hbm],
        out_specs=[hbm, vmem, vmem],
        out_shape=[
            jax.ShapeDtypeStruct((ff, 2 * slots), bf16),
            jax.ShapeDtypeStruct((8, 2 * slots), f32),
            jax.ShapeDtypeStruct((8, 2 * slots), f32),
        ],
        scratch_shapes=[
            pltpu.VMEM((2, slots, width), f32),
            pltpu.VMEM((2, slots, width), bf16),
            pltpu.VMEM((2, slots, 128), f32),
            pltpu.VMEM((blocks * META, top * tok), f32),
            pltpu.VMEM((ff, width), bf16),
            pltpu.VMEM((ff, 2 * slots), bf16),
            pltpu.VMEM((ff, 2 * slots), bf16),
            pltpu.SemaphoreType.DMA((tiles,)),
            pltpu.SemaphoreType.DMA((tiles,)),
            pltpu.SemaphoreType.DMA((tiles,)),
        ],
        compiler_params=pltpu.CompilerParams(vmem_limit_bytes=50 * 1024 * 1024),
        cost_estimate=pl.CostEstimate(
            flops=4 * ff * width * slots, bytes_accessed=16 * 1024 * 1024, transcendentals=0
        ),
    )(info, *msgs, down_weight.reshape(ff, width), saved_all)

    terms = lax.psum_scatter(partial, "dp", scatter_dimension=0, tiled=True)
    slot_grad = lax.psum(jnp.sum(slot_part, axis=0), "dp")
    home = jnp.transpose(slot_grad.reshape(2, blocks, cap), (1, 0, 2)).reshape(blocks, 2 * cap)
    back = lax.all_to_all(home, "expert", split_axis=0, concat_axis=0, tiled=True)
    logits = pl.pallas_call(
        functools.partial(logits_kernel, cap),
        out_shape=[jax.ShapeDtypeStruct((top, tok), f32)] * 2,
        scratch_shapes=[pltpu.VMEM((top, tok), f32)],
    )(*side, back)
    hidden = []
    for m in range(2):
        cols = slice(m * slots, (m + 1) * slots)
        scaled = (gates[:1, cols] * terms[:, cols].astype(f32)).astype(bf16)
        hidden.append(scaled.reshape(1, ff_shard, 1, slots))
    return (*hidden, *(g.T[None] for g in logits))


def solution(mesh):
    in_specs = (
        P("section", "expert", "dp"),
        P("section", "expert", "dp"),
        P("section", "expert", None),
        P("section", "expert", None),
        P("section", "expert", None),
        P("section", "expert", None),
        P("section", "expert", None, "dp"),
        P("section", "dp", "expert", None),
        P("section", "dp", "expert", None),
    )
    out_specs = (
        P("section", "dp", "expert", None),
        P("section", "dp", "expert", None),
        P("section", "expert", None),
        P("section", "expert", None),
    )
    return jax.shard_map(shards, mesh=mesh, in_specs=in_specs, out_specs=out_specs, check_vma=False)
```

```python
import functools

import jax
import jax.numpy as jnp
from jax import lax
from jax.experimental import pallas as pl
from jax.experimental.pallas import tpu as pltpu
from jax.sharding import PartitionSpec as P

route_scale = 2.5
META = 8
NT = (((1,), (1,)), ((), ()))
f32 = jnp.float32
bf16 = jnp.bfloat16


def pack_kernel(rf, sf, rr, sr, out, buf):
    top, tok = rf.shape
    buf[...] = jnp.zeros_like(buf)
    for m, (routes, scores) in enumerate(((rf, sf), (rr, sr))):
        ids = routes[...].astype(f32)
        s = scores[...]
        gate = route_scale * s / jnp.sum(s, axis=0, keepdims=True)
        for k in range(top):
            buf[2 * m : 2 * m + 1, k * tok : (k + 1) * tok] = ids[k : k + 1]
            buf[2 * m + 1 : 2 * m + 2, k * tok : (k + 1) * tok] = gate[k : k + 1]
    out[...] = buf[...].astype(out.dtype)


def saved_kernel(half, info, first, second, out):
    for m, ref in enumerate((first, second)):
        turned = pltpu.roll(ref[...].astype(f32), info[3], 1).astype(out.dtype)
        for h in range(2):
            at = (2 * h + m) * half
            out[:, at : at + half] = turned[:, h * half : (h + 1) * half]


def hidden_kernel(half, info, terms, gate_0, gate_1, first, second):
    for m, out in enumerate((first, second)):
        low, high = slice(m * half, (m + 1) * half), slice((2 + m) * half, (3 + m) * half)
        x = jnp.concatenate([terms[:, low], terms[:, high]], axis=1).astype(f32)
        gate = jnp.concatenate([gate_0[0:1, low], gate_1[0:1, low]], axis=1)
        out[...] = pltpu.roll(x * gate, info[2], 1).astype(out.dtype)


def expert_kernel(blocks, tok, top, cap, half, info, *refs):
    msgs = refs[:blocks]
    refs = refs[blocks:]
    w_hbm, saved_hbm = refs[:2]
    part_hbm, slot_ref, gate_ref, rows16, gcol, meta, w_ref, saved_ref, part_ref, w_sem, saved_sem, part_sem = refs[-12:]
    slots = blocks * cap
    lanes = 2 * tok
    tiles = w_sem.shape[0]
    tile = w_ref.shape[0] // tiles
    columns = pl.ds(half * 2 * slots, 2 * slots)
    parts = [pl.ds(i * tile, tile) for i in range(tiles)]
    fetched = []
    for i, at in enumerate(parts):
        pair = (
            pltpu.make_async_copy(w_hbm.at[at], w_ref.at[at], w_sem.at[i]),
            pltpu.make_async_copy(saved_hbm.at[at, columns], saved_ref.at[at], saved_sem.at[i]),
        )
        for copy in pair:
            copy.start()
        fetched.append(pair)

    for b in range(blocks):
        meta[b * META : (b + 1) * META, :] = msgs[b][lanes : lanes + META, : top * tok].astype(f32)
    vals = meta[...]
    mine = (vals == info[0].astype(f32)).astype(f32)
    t_in = lax.rem(lax.broadcasted_iota(jnp.int32, (top * tok, lanes), 0), tok)
    t_out = lax.rem(lax.broadcasted_iota(jnp.int32, (top * tok, lanes), 1), tok)
    same = (t_in == t_out).astype(f32).astype(bf16)
    before = (t_in < t_out).astype(f32).astype(bf16)
    hot = mine.astype(bf16)
    named = jnp.dot(hot, same, preferred_element_type=f32)
    place = jnp.dot(hot, before, preferred_element_type=f32)
    picked = (pltpu.roll(mine, 1, 0) * vals).astype(bf16)
    gates = jnp.dot(picked, same, preferred_element_type=f32)
    rising = lax.broadcasted_iota(jnp.int32, (1, lanes), 1) >= tok
    shift = jnp.where(rising, float(cap), 0.0)
    slot_id = lax.broadcasted_iota(jnp.int32, (2 * cap, lanes), 0).astype(f32)
    swapped = info[1] == 1
    for p in range(blocks // 2):
        got, col = [], []
        for b in (2 * p, 2 * p + 1):
            r = b * META
            name = jnp.where(rising, named[r + 2 : r + 3], named[r : r + 1])
            pos = jnp.where(rising, place[r + 2 : r + 3], place[r : r + 1])
            gate = jnp.where(rising, gates[r + 3 : r + 4], gates[r + 1 : r + 2])
            target = jnp.where(name > 0.5, pos + shift, -1.0)
            put = (slot_id == target).astype(f32)
            got.append(jnp.dot(put.astype(bf16), msgs[b][:lanes, :], preferred_element_type=f32))
            col.append(jnp.broadcast_to(jnp.sum(put * gate, axis=1, keepdims=True), (2 * cap, gcol.shape[1])))
        for array, ref in ((got, rows16), (col, gcol)):
            low = jnp.where(swapped, array[1], array[0])
            high = jnp.where(swapped, array[0], array[1])
            for m in range(2):
                at, take = m * slots + 2 * p * cap, slice(m * cap, (m + 1) * cap)
                ref[at : at + 2 * cap, :] = jnp.concatenate([low[take], high[take]], axis=0).astype(bf16)
    first = (lax.broadcasted_iota(jnp.int32, (8, gcol.shape[1]), 1) == 0).astype(f32).astype(bf16)
    gate_ref[...] = lax.dot_general(first, gcol[...], NT, preferred_element_type=f32)

    sent = []
    for i, at in enumerate(parts):
        for copy in fetched[i]:
            copy.wait()
        part = lax.dot_general(w_ref[at, :], rows16[...], NT, preferred_element_type=f32).astype(bf16)
        part_ref[at, :] = part
        prod = part.astype(f32) * saved_ref[at, :].astype(f32)
        total = jnp.sum(prod.reshape(-1, 8, 2 * slots), axis=0)
        slot_ref[...] = total if i == 0 else slot_ref[...] + total
        copy = pltpu.make_async_copy(part_ref.at[at], part_hbm.at[at, columns], part_sem.at[i])
        copy.start()
        sent.append(copy)
    for copy in sent:
        copy.wait()


def logits_kernel(cap, rf, sf, rr, sr, back, out_f, out_r, grad):
    top, tok = rf.shape
    experts = back.shape[0]
    ids = lax.broadcasted_iota(jnp.int32, (experts, tok), 0)
    t0 = lax.broadcasted_iota(jnp.int32, (tok, tok), 0)
    t1 = lax.broadcasted_iota(jnp.int32, (tok, tok), 1)
    before = (t0 < t1).astype(f32).astype(bf16)
    for m, (routes, scores, out) in enumerate(((rf, sf, out_f), (rr, sr, out_r))):
        named = jnp.zeros((experts, tok), f32)
        for k in range(top):
            named += (routes[k : k + 1, :] == ids).astype(f32)
        place = jnp.dot(named.astype(bf16), before, preferred_element_type=f32)
        vals = jnp.zeros((experts, tok), f32)
        for c in range(cap):
            vals += jnp.where(place == float(c), back[:, m * cap + c : m * cap + c + 1], 0.0)
        for k in range(top):
            chosen = jnp.where(routes[k : k + 1, :] == ids, vals, 0.0)
            grad[k : k + 1, :] = jnp.sum(chosen, axis=0, keepdims=True)
        s = scores[...]
        total = jnp.sum(s, axis=0, keepdims=True)
        mean = jnp.sum(grad[...] * s, axis=0, keepdims=True) / total
        out[...] = route_scale / total * (grad[...] - mean) * s * (1.0 - s)


def shards(
    falling_grad,
    rising_grad,
    routes_falling,
    routes_rising,
    scores_falling,
    scores_rising,
    down_weight,
    saved_falling,
    saved_rising,
):
    blocks = lax.axis_size("expert")
    sections = lax.axis_size("section")
    dp = lax.axis_size("dp")
    tok, width = falling_grad.shape[1:]
    top = routes_falling.shape[2]
    ff_shard, slots = saved_falling.shape[1], saved_falling.shape[3]
    cap = slots // blocks
    ff = ff_shard * dp
    depth = blocks // 2
    lanes = 2 * tok

    side = (
        routes_falling[0].T,
        scores_falling[0].T,
        routes_rising[0].T,
        scores_rising[0].T,
    )
    me = lax.axis_index("expert")
    level, column = me // 2, me % 2
    turn = (level + depth - 1) % depth
    group = slots // 2
    info = jnp.stack(
        [me, column, turn * 2 * cap, (depth - turn) % depth * 2 * cap]
    ).astype(jnp.int32)
    smem = pl.BlockSpec(memory_space=pltpu.SMEM)
    vmem = pl.BlockSpec(memory_space=pltpu.VMEM)
    hbm = pl.BlockSpec(memory_space=pltpu.HBM)

    def hop(array, by, flip):
        pairs = [
            (s * blocks + e, (s + by) % sections * blocks + (e ^ flip))
            for s in range(sections)
            for e in range(blocks)
        ]
        return lax.ppermute(array, ("section", "expert"), pairs)

    own_f, own_r = hop(falling_grad[0], -1, 0), hop(rising_grad[0], 1, 0)
    meta = pl.pallas_call(
        pack_kernel,
        out_shape=jax.ShapeDtypeStruct((META, width), bf16),
        scratch_shapes=[pltpu.VMEM((META, width), f32)],
    )(*side)
    own = jnp.concatenate([own_f, own_r, meta], axis=0)
    far = hop(own, 0, 1)

    saved = pl.pallas_call(
        functools.partial(saved_kernel, group),
        in_specs=[smem, vmem, vmem],
        out_specs=vmem,
        out_shape=jax.ShapeDtypeStruct((ff_shard, 2 * slots), bf16),
    )(info, saved_falling.reshape(ff_shard, slots), saved_rising.reshape(ff_shard, slots))
    own_ring, saved = lax.optimization_barrier((own, saved))
    saved_all = lax.all_gather(saved, "dp", tiled=True)

    up = [(i, (i + 2) % blocks) for i in range(blocks)]
    down = [(i, (i - 2) % blocks) for i in range(blocks)]
    half = depth // 2
    near, away = {0: own}, {0: far}
    near[-1] = lax.ppermute(own_ring, "expert", up)
    near[1] = lax.ppermute(own_ring, "expert", down)
    near[-1], near[1], away[0] = lax.optimization_barrier((near[-1], near[1], far))
    for t in range(1, half + 1):
        if t > 1:
            near[-t] = lax.ppermute(near[1 - t], "expert", up)
        if 1 < t < half:
            near[t] = lax.ppermute(near[t - 1], "expert", down)
        if t < half:
            away[-t] = lax.ppermute(away[1 - t], "expert", up)
        away[t] = lax.ppermute(away[t - 1], "expert", down)
    near[half] = near[-half]

    tiles = max(1, ff // 256)

    def multiply(part, levels, held):
        msgs = [side[r if r <= half else r - depth] for r in levels for side in (near, away)]
        blocks = len(msgs)
        width_out = 2 * blocks * cap
        return pl.pallas_call(
            functools.partial(expert_kernel, blocks, tok, top, cap, part),
            in_specs=[smem] + [vmem] * blocks + [hbm, hbm] + [hbm] * len(held),
            out_specs=[hbm, vmem, vmem],
            out_shape=[
                jax.ShapeDtypeStruct((ff, 2 * slots), bf16),
                jax.ShapeDtypeStruct((8, width_out), f32),
                jax.ShapeDtypeStruct((8, width_out), f32),
            ],
            input_output_aliases={blocks + 3: 0} if held else {},
            scratch_shapes=[
                pltpu.VMEM((width_out, width), bf16),
                pltpu.VMEM((width_out, 128), bf16),
                pltpu.VMEM((blocks * META, top * tok), f32),
                pltpu.VMEM((ff, width), bf16),
                pltpu.VMEM((ff, width_out), bf16),
                pltpu.VMEM((ff, width_out), bf16),
                pltpu.SemaphoreType.DMA((tiles,)),
                pltpu.SemaphoreType.DMA((tiles,)),
                pltpu.SemaphoreType.DMA((tiles,)),
            ],
            compiler_params=pltpu.CompilerParams(vmem_limit_bytes=50 * 1024 * 1024),
            cost_estimate=pl.CostEstimate(
                flops=2 * ff * width * slots, bytes_accessed=8 * 1024 * 1024, transcendentals=0
            ),
        )(info, *msgs, down_weight.reshape(ff, width), saved_all, *held)

    partial, slot_0, gate_0 = multiply(0, (-1, 0, 1, 2), ())
    partial, slot_1, gate_1 = multiply(1, (3, 4, 5, 6), (partial,))

    terms = lax.psum_scatter(partial, "dp", scatter_dimension=0, tiled=True)
    slot_part = jnp.stack([slot_0, slot_1], axis=1).reshape(8, 2, 2, group)
    slot_part = jnp.moveaxis(jnp.sum(slot_part, axis=0), 0, 1).reshape(2, slots)
    slot_grad = lax.psum(slot_part, "dp")
    slot_grad = jnp.roll(slot_grad, info[2], axis=1)
    home = jnp.transpose(slot_grad.reshape(2, blocks, cap), (1, 0, 2)).reshape(blocks, 2 * cap)
    back = lax.all_to_all(home, "expert", split_axis=0, concat_axis=0, tiled=True)
    logits = pl.pallas_call(
        functools.partial(logits_kernel, cap),
        out_shape=[jax.ShapeDtypeStruct((top, tok), f32)] * 2,
        scratch_shapes=[pltpu.VMEM((top, tok), f32)],
    )(*side, back)
    hidden = pl.pallas_call(
        functools.partial(hidden_kernel, group),
        in_specs=[smem, vmem, vmem, vmem],
        out_specs=[vmem, vmem],
        out_shape=[jax.ShapeDtypeStruct((ff_shard, slots), bf16)] * 2,
    )(info, terms, gate_0, gate_1)
    hidden = [h.reshape(1, ff_shard, 1, slots) for h in hidden]
    return (*hidden, *(g.T[None] for g in logits))


def solution(mesh):
    in_specs = (
        P("section", "expert", "dp"),
        P("section", "expert", "dp"),
        P("section", "expert", None),
        P("section", "expert", None),
        P("section", "expert", None),
        P("section", "expert", None),
        P("section", "expert", None, "dp"),
        P("section", "dp", "expert", None),
        P("section", "dp", "expert", None),
    )
    out_specs = (
        P("section", "dp", "expert", None),
        P("section", "dp", "expert", None),
        P("section", "expert", None),
        P("section", "expert", None),
    )
    return jax.shard_map(shards, mesh=mesh, in_specs=in_specs, out_specs=out_specs, check_vma=False)
```

```python
import functools

import jax
import jax.numpy as jnp
from jax import lax
from jax.experimental import pallas as pl
from jax.experimental.pallas import tpu as pltpu
from jax.sharding import PartitionSpec as P

route_scale = 2.5
META = 8
NT = (((1,), (1,)), ((), ()))
f32 = jnp.float32
bf16 = jnp.bfloat16


def pack_kernel(rf, sf, rr, sr, out, buf):
    top, tok = rf.shape
    buf[...] = jnp.zeros_like(buf)
    for m, (routes, scores) in enumerate(((rf, sf), (rr, sr))):
        ids = routes[...].astype(f32)
        s = scores[...]
        gate = route_scale * s / jnp.sum(s, axis=0, keepdims=True)
        for k in range(top):
            buf[2 * m : 2 * m + 1, k * tok : (k + 1) * tok] = ids[k : k + 1]
            buf[2 * m + 1 : 2 * m + 2, k * tok : (k + 1) * tok] = gate[k : k + 1]
    out[...] = buf[...].astype(out.dtype)


def placements(msgs, tok, top, cap, expert, meta):
    blocks, lanes = len(msgs), 2 * tok
    for b in range(blocks):
        meta[b * META : (b + 1) * META, :] = msgs[b][lanes : lanes + META, : top * tok].astype(f32)
    vals = meta[...]
    mine = (vals == expert.astype(f32)).astype(f32)
    t_in = lax.rem(lax.broadcasted_iota(jnp.int32, (top * tok, lanes), 0), tok)
    t_out = lax.rem(lax.broadcasted_iota(jnp.int32, (top * tok, lanes), 1), tok)
    same = (t_in == t_out).astype(f32).astype(bf16)
    before = (t_in < t_out).astype(f32).astype(bf16)
    hot = mine.astype(bf16)
    named = jnp.dot(hot, same, preferred_element_type=f32)
    place = jnp.dot(hot, before, preferred_element_type=f32)
    picked = (pltpu.roll(mine, 1, 0) * vals).astype(bf16)
    gates = jnp.dot(picked, same, preferred_element_type=f32)
    rising = lax.broadcasted_iota(jnp.int32, (1, lanes), 1) >= tok
    shift = jnp.where(rising, float(cap), 0.0)
    slot_id = lax.broadcasted_iota(jnp.int32, (2 * cap, lanes), 0).astype(f32)
    result = []
    for b in range(blocks):
        r = b * META
        name = jnp.where(rising, named[r + 2 : r + 3], named[r : r + 1])
        pos = jnp.where(rising, place[r + 2 : r + 3], place[r : r + 1])
        gate = jnp.where(rising, gates[r + 3 : r + 4], gates[r + 1 : r + 2])
        target = jnp.where(name > 0.5, pos + shift, -1.0)
        result.append(((slot_id == target).astype(f32), gate))
    return result


def early_kernel(blocks, tok, top, cap, info, *refs):
    msgs, (out, meta) = refs[:blocks], refs[blocks:]
    for b, (put, _) in enumerate(placements(msgs, tok, top, cap, info[0], meta)):
        got = jnp.dot(put.astype(bf16), msgs[b][: 2 * tok, :], preferred_element_type=f32)
        out[b * 2 * cap : (b + 1) * 2 * cap, :] = got.astype(bf16)


def expert_kernel(blocks, early, tok, top, cap, info, *refs):
    msgs = refs[:blocks]
    done_ref, w_hbm, saved_hbm, part_hbm, slot_ref, gate_ref = refs[blocks : blocks + 6]
    rows, rows16, gcol, meta, w_ref, saved_ref, part_ref, w_sem, saved_sem, part_sem = refs[blocks + 6 :]
    slots = blocks * cap
    tiles = saved_sem.shape[0]
    tile = w_ref.shape[0] // tiles
    parts = [pl.ds(i * tile, tile) for i in range(tiles)]
    fetched = []
    for i, at in enumerate(parts):
        pair = (
            pltpu.make_async_copy(w_hbm.at[at], w_ref.at[at], w_sem.at[i]),
            pltpu.make_async_copy(saved_hbm.at[at], saved_ref.at[at], saved_sem.at[i]),
        )
        for copy in pair:
            copy.start()
        fetched.append(pair)

    for b, (put, gate) in enumerate(placements(msgs, tok, top, cap, info[0], meta)):
        if b < early:
            got = done_ref[b * 2 * cap : (b + 1) * 2 * cap, :].astype(f32)
        else:
            got = jnp.dot(put.astype(bf16), msgs[b][: 2 * tok, :], preferred_element_type=f32)
        col = jnp.broadcast_to(jnp.sum(put * gate, axis=1, keepdims=True), (2 * cap, gcol.shape[2]))
        at = pl.ds(pl.multiple_of(info[1 + b] * cap, 8), cap)
        for m in range(2):
            rows[m, at, :] = got[m * cap : (m + 1) * cap]
            gcol[m, at, :] = col[m * cap : (m + 1) * cap]
    first = (lax.broadcasted_iota(jnp.int32, (8, gcol.shape[2]), 1) == 0).astype(f32).astype(bf16)
    for m in range(2):
        cols = slice(m * slots, (m + 1) * slots)
        rows16[cols, :] = rows[m].astype(bf16)
        gate_ref[:, cols] = lax.dot_general(first, gcol[m].astype(bf16), NT, preferred_element_type=f32)

    sent = []
    for i, at in enumerate(parts):
        fetched[i][0].wait()
        part = lax.dot_general(w_ref[at, :], rows16[...], NT, preferred_element_type=f32).astype(bf16)
        part_ref[at, :] = part
        copy = pltpu.make_async_copy(part_ref.at[at], part_hbm.at[at], part_sem.at[i])
        copy.start()
        sent.append(copy)
        fetched[i][1].wait()
        prod = part.astype(f32) * saved_ref[at, :].astype(f32)
        total = jnp.sum(prod.reshape(-1, 8, 2 * slots), axis=0)
        slot_ref[...] = total if i == 0 else slot_ref[...] + total
    for copy in sent:
        copy.wait()


def logits_kernel(cap, rf, sf, rr, sr, back, out_f, out_r, grad):
    top, tok = rf.shape
    experts = back.shape[0]
    ids = lax.broadcasted_iota(jnp.int32, (experts, tok), 0)
    t0 = lax.broadcasted_iota(jnp.int32, (tok, tok), 0)
    t1 = lax.broadcasted_iota(jnp.int32, (tok, tok), 1)
    before = (t0 < t1).astype(f32).astype(bf16)
    for m, (routes, scores, out) in enumerate(((rf, sf, out_f), (rr, sr, out_r))):
        named = jnp.zeros((experts, tok), f32)
        for k in range(top):
            named += (routes[k : k + 1, :] == ids).astype(f32)
        place = jnp.dot(named.astype(bf16), before, preferred_element_type=f32)
        vals = jnp.zeros((experts, tok), f32)
        for c in range(cap):
            vals += jnp.where(place == float(c), back[:, m * cap + c : m * cap + c + 1], 0.0)
        for k in range(top):
            chosen = jnp.where(routes[k : k + 1, :] == ids, vals, 0.0)
            grad[k : k + 1, :] = jnp.sum(chosen, axis=0, keepdims=True)
        s = scores[...]
        total = jnp.sum(s, axis=0, keepdims=True)
        mean = jnp.sum(grad[...] * s, axis=0, keepdims=True) / total
        out[...] = route_scale / total * (grad[...] - mean) * s * (1.0 - s)


def shards(
    falling_grad,
    rising_grad,
    routes_falling,
    routes_rising,
    scores_falling,
    scores_rising,
    down_weight,
    saved_falling,
    saved_rising,
):
    blocks = lax.axis_size("expert")
    sections = lax.axis_size("section")
    dp = lax.axis_size("dp")
    tok, width = falling_grad.shape[1:]
    top = routes_falling.shape[2]
    ff_shard, slots = saved_falling.shape[1], saved_falling.shape[3]
    cap = slots // blocks
    ff = ff_shard * dp
    depth = blocks // 2
    lanes = 2 * tok

    side = (
        routes_falling[0].T,
        scores_falling[0].T,
        routes_rising[0].T,
        scores_rising[0].T,
    )
    def hop(array, by, flip):
        pairs = [
            (s * blocks + e, (s + by) % sections * blocks + (e ^ flip))
            for s in range(sections)
            for e in range(blocks)
        ]
        return lax.ppermute(array, ("section", "expert"), pairs)

    own_f, own_r = hop(falling_grad[0], -1, 0), hop(rising_grad[0], 1, 0)
    meta = pl.pallas_call(
        pack_kernel,
        out_shape=jax.ShapeDtypeStruct((META, width), bf16),
        scratch_shapes=[pltpu.VMEM((META, width), f32)],
    )(*side)
    own = jnp.concatenate([own_f, own_r, meta], axis=0)
    far = hop(own, 0, 1)

    saved = jnp.concatenate(
        [saved_falling.reshape(ff_shard, slots), saved_rising.reshape(ff_shard, slots)], axis=1
    )
    own_ring, saved = lax.optimization_barrier((own, saved))
    saved_all = lax.all_gather(saved, "dp", tiled=True)

    up = [(i, (i + 2) % blocks) for i in range(blocks)]
    down = [(i, (i - 2) % blocks) for i in range(blocks)]
    me = lax.axis_index("expert")
    level, column = me // 2, me % 2
    msgs, index = [own, far], [me, level * 2 + 1 - column]

    def step(rise, fall, side, t):
        if rise is not None:
            rise = lax.ppermute(rise, "expert", up)
            msgs.append(rise)
            index.append((level - t) % depth * 2 + side)
        if fall is not None:
            fall = lax.ppermute(fall, "expert", down)
            msgs.append(fall)
            index.append((level + t) % depth * 2 + side)
        return rise, fall

    half = depth // 2
    own_rise = own_fall = own_ring
    for t in range(1, half):
        own_rise, own_fall = step(own_rise, own_fall, column, t)
        if t == 1:
            own_rise, own_fall, far = lax.optimization_barrier((own_rise, own_fall, far))
            msgs[1:] = far, own_rise, own_fall
    step(own_rise, None, column, half)
    far_rise = far_fall = far
    for t in range(1, half):
        far_rise, far_fall = step(far_rise, far_fall, 1 - column, t)
    step(None, far_fall, 1 - column, half)
    late = (7, 8, 13, 14, 15)
    order = [i for i in range(blocks) if i not in late] + list(late)
    early = blocks - len(late)
    msgs = [msgs[i] for i in order]
    info = jnp.stack([me] + [index[i] for i in order]).astype(jnp.int32)

    tiles = max(1, ff // 256)
    smem, vmem = pl.BlockSpec(memory_space=pltpu.SMEM), pl.BlockSpec(memory_space=pltpu.VMEM)
    hbm = pl.BlockSpec(memory_space=pltpu.HBM)
    done = pl.pallas_call(
        functools.partial(early_kernel, early, tok, top, cap),
        in_specs=[smem] + [vmem] * early,
        out_specs=vmem,
        out_shape=jax.ShapeDtypeStruct((early * 2 * cap, width), bf16),
        scratch_shapes=[pltpu.VMEM((early * META, top * tok), f32)],
        compiler_params=pltpu.CompilerParams(vmem_limit_bytes=32 * 1024 * 1024),
        cost_estimate=pl.CostEstimate(
            flops=4 * ff * width * slots, bytes_accessed=8 * 1024 * 1024, transcendentals=0
        ),
    )(info, *msgs[:early])
    partial, slot_part, gates = pl.pallas_call(
        functools.partial(expert_kernel, blocks, early, tok, top, cap),
        in_specs=[smem] + [vmem] * blocks + [vmem, hbm, hbm],
        out_specs=[hbm, vmem, vmem],
        out_shape=[
            jax.ShapeDtypeStruct((ff, 2 * slots), bf16),
            jax.ShapeDtypeStruct((8, 2 * slots), f32),
            jax.ShapeDtypeStruct((8, 2 * slots), f32),
        ],
        scratch_shapes=[
            pltpu.VMEM((2, slots, width), f32),
            pltpu.VMEM((2 * slots, width), bf16),
            pltpu.VMEM((2, slots, 128), f32),
            pltpu.VMEM((blocks * META, top * tok), f32),
            pltpu.VMEM((ff, width), bf16),
            pltpu.VMEM((ff, 2 * slots), bf16),
            pltpu.VMEM((ff, 2 * slots), bf16),
            pltpu.SemaphoreType.DMA((tiles,)),
            pltpu.SemaphoreType.DMA((tiles,)),
            pltpu.SemaphoreType.DMA((tiles,)),
        ],
        compiler_params=pltpu.CompilerParams(vmem_limit_bytes=48 * 1024 * 1024),
        cost_estimate=pl.CostEstimate(
            flops=4 * ff * width * slots, bytes_accessed=16 * 1024 * 1024, transcendentals=0
        ),
    )(info, *msgs, done, down_weight.reshape(ff, width), saved_all)

    terms = lax.psum_scatter(partial, "dp", scatter_dimension=0, tiled=True)
    slot_grad = lax.psum(jnp.sum(slot_part, axis=0), "dp")
    home = jnp.transpose(slot_grad.reshape(2, blocks, cap), (1, 0, 2)).reshape(blocks, 2 * cap)
    back = lax.all_to_all(home, "expert", split_axis=0, concat_axis=0, tiled=True)
    logits = pl.pallas_call(
        functools.partial(logits_kernel, cap),
        out_shape=[jax.ShapeDtypeStruct((top, tok), f32)] * 2,
        scratch_shapes=[pltpu.VMEM((top, tok), f32)],
    )(*side, back)
    hidden = []
    for m in range(2):
        cols = slice(m * slots, (m + 1) * slots)
        scaled = (gates[:1, cols] * terms[:, cols].astype(f32)).astype(bf16)
        hidden.append(scaled.reshape(1, ff_shard, 1, slots))
    return (*hidden, *(g.T[None] for g in logits))


def solution(mesh):
    in_specs = (
        P("section", "expert", "dp"),
        P("section", "expert", "dp"),
        P("section", "expert", None),
        P("section", "expert", None),
        P("section", "expert", None),
        P("section", "expert", None),
        P("section", "expert", None, "dp"),
        P("section", "dp", "expert", None),
        P("section", "dp", "expert", None),
    )
    out_specs = (
        P("section", "dp", "expert", None),
        P("section", "dp", "expert", None),
        P("section", "expert", None),
        P("section", "expert", None),
    )
    return jax.shard_map(shards, mesh=mesh, in_specs=in_specs, out_specs=out_specs, check_vma=False)
```

```python
import functools

import jax
import jax.numpy as jnp
from jax import lax
from jax.experimental import pallas as pl
from jax.experimental.pallas import tpu as pltpu
from jax.sharding import PartitionSpec as P

route_scale = 2.5
META = 8
NT = (((1,), (1,)), ((), ()))
f32 = jnp.float32
bf16 = jnp.bfloat16


def pack_kernel(rf, sf, rr, sr, out, buf):
    top, tok = rf.shape
    buf[...] = jnp.zeros_like(buf)
    for m, (routes, scores) in enumerate(((rf, sf), (rr, sr))):
        ids = routes[...].astype(f32)
        s = scores[...]
        gate = route_scale * s / jnp.sum(s, axis=0, keepdims=True)
        for k in range(top):
            buf[2 * m : 2 * m + 1, k * tok : (k + 1) * tok] = ids[k : k + 1]
            buf[2 * m + 1 : 2 * m + 2, k * tok : (k + 1) * tok] = gate[k : k + 1]
    out[...] = buf[...].astype(out.dtype)


def expert_kernel(blocks, tok, top, cap, info, *refs):
    msgs = refs[:blocks]
    rows16, gate_ref, rows, gcol, meta = refs[blocks:]
    slots = blocks * cap
    lanes = 2 * tok

    for b in range(blocks):
        meta[b * META : (b + 1) * META, :] = msgs[b][lanes : lanes + META, : top * tok].astype(f32)
    vals = meta[...]
    mine = (vals == info[0].astype(f32)).astype(f32)
    t_in = lax.rem(lax.broadcasted_iota(jnp.int32, (top * tok, lanes), 0), tok)
    t_out = lax.rem(lax.broadcasted_iota(jnp.int32, (top * tok, lanes), 1), tok)
    same = (t_in == t_out).astype(f32).astype(bf16)
    before = (t_in < t_out).astype(f32).astype(bf16)
    hot = mine.astype(bf16)
    named = jnp.dot(hot, same, preferred_element_type=f32)
    place = jnp.dot(hot, before, preferred_element_type=f32)
    picked = (pltpu.roll(mine, 1, 0) * vals).astype(bf16)
    gates = jnp.dot(picked, same, preferred_element_type=f32)
    rising = lax.broadcasted_iota(jnp.int32, (1, lanes), 1) >= tok
    shift = jnp.where(rising, float(cap), 0.0)
    slot_id = lax.broadcasted_iota(jnp.int32, (2 * cap, lanes), 0).astype(f32)
    for b in range(blocks):
        r = b * META
        name = jnp.where(rising, named[r + 2 : r + 3], named[r : r + 1])
        pos = jnp.where(rising, place[r + 2 : r + 3], place[r : r + 1])
        gate = jnp.where(rising, gates[r + 3 : r + 4], gates[r + 1 : r + 2])
        target = jnp.where(name > 0.5, pos + shift, -1.0)
        put = (slot_id == target).astype(f32)
        got = jnp.dot(put.astype(bf16), msgs[b][:lanes, :], preferred_element_type=f32)
        col = jnp.broadcast_to(jnp.sum(put * gate, axis=1, keepdims=True), (2 * cap, gcol.shape[2]))
        at = pl.ds(pl.multiple_of(info[1 + b] * cap, 8), cap)
        for m in range(2):
            rows[m, at, :] = got[m * cap : (m + 1) * cap]
            gcol[m, at, :] = col[m * cap : (m + 1) * cap]
    first = (lax.broadcasted_iota(jnp.int32, (8, gcol.shape[2]), 1) == 0).astype(f32).astype(bf16)
    for m in range(2):
        rows16[m * slots : (m + 1) * slots, :] = rows[m].astype(bf16)
        gate_ref[:, m * slots : (m + 1) * slots] = lax.dot_general(
            first, gcol[m].astype(bf16), NT, preferred_element_type=f32
        )


def logits_kernel(cap, rf, sf, rr, sr, back, out_f, out_r, grad):
    top, tok = rf.shape
    experts = back.shape[0]
    ids = lax.broadcasted_iota(jnp.int32, (experts, tok), 0)
    t0 = lax.broadcasted_iota(jnp.int32, (tok, tok), 0)
    t1 = lax.broadcasted_iota(jnp.int32, (tok, tok), 1)
    before = (t0 < t1).astype(f32).astype(bf16)
    for m, (routes, scores, out) in enumerate(((rf, sf, out_f), (rr, sr, out_r))):
        named = jnp.zeros((experts, tok), f32)
        for k in range(top):
            named += (routes[k : k + 1, :] == ids).astype(f32)
        place = jnp.dot(named.astype(bf16), before, preferred_element_type=f32)
        vals = jnp.zeros((experts, tok), f32)
        for c in range(cap):
            vals += jnp.where(place == float(c), back[:, m * cap + c : m * cap + c + 1], 0.0)
        for k in range(top):
            chosen = jnp.where(routes[k : k + 1, :] == ids, vals, 0.0)
            grad[k : k + 1, :] = jnp.sum(chosen, axis=0, keepdims=True)
        s = scores[...]
        total = jnp.sum(s, axis=0, keepdims=True)
        mean = jnp.sum(grad[...] * s, axis=0, keepdims=True) / total
        out[...] = route_scale / total * (grad[...] - mean) * s * (1.0 - s)


def shards(
    falling_grad,
    rising_grad,
    routes_falling,
    routes_rising,
    scores_falling,
    scores_rising,
    down_weight,
    saved_falling,
    saved_rising,
):
    blocks = lax.axis_size("expert")
    sections = lax.axis_size("section")
    dp = lax.axis_size("dp")
    tok, width = falling_grad.shape[1:]
    top = routes_falling.shape[2]
    ff_shard, slots = saved_falling.shape[1], saved_falling.shape[3]
    cap = slots // blocks
    ff = ff_shard * dp
    depth = blocks // 2
    lanes = 2 * tok

    side = (
        routes_falling[0].T,
        scores_falling[0].T,
        routes_rising[0].T,
        scores_rising[0].T,
    )
    def hop(array, by, flip):
        pairs = [
            (s * blocks + e, (s + by) % sections * blocks + (e ^ flip))
            for s in range(sections)
            for e in range(blocks)
        ]
        return lax.ppermute(array, ("section", "expert"), pairs)

    own_f, own_r = hop(falling_grad[0], -1, 0), hop(rising_grad[0], 1, 0)
    meta = pl.pallas_call(
        pack_kernel,
        out_shape=jax.ShapeDtypeStruct((META, width), bf16),
        scratch_shapes=[pltpu.VMEM((META, width), f32)],
    )(*side)
    own = jnp.concatenate([own_f, own_r, meta], axis=0)
    far = hop(own, 0, 1)

    saved = jnp.concatenate(
        [saved_falling.reshape(ff_shard, slots), saved_rising.reshape(ff_shard, slots)], axis=1
    )
    own_ring, saved = lax.optimization_barrier((own, saved))
    saved_all = lax.all_gather(saved, "dp", tiled=True)

    up = [(i, (i + 2) % blocks) for i in range(blocks)]
    down = [(i, (i - 2) % blocks) for i in range(blocks)]
    me = lax.axis_index("expert")
    level, column = me // 2, me % 2
    msgs, index = [own, far], [me, level * 2 + 1 - column]

    def step(rise, fall, side, t):
        if rise is not None:
            rise = lax.ppermute(rise, "expert", up)
            msgs.append(rise)
            index.append((level - t) % depth * 2 + side)
        if fall is not None:
            fall = lax.ppermute(fall, "expert", down)
            msgs.append(fall)
            index.append((level + t) % depth * 2 + side)
        return rise, fall

    half = depth // 2
    own_rise = own_fall = own_ring
    for t in range(1, half):
        own_rise, own_fall = step(own_rise, own_fall, column, t)
        if t == 1:
            own_rise, own_fall, far = lax.optimization_barrier((own_rise, own_fall, far))
            msgs[1:] = far, own_rise, own_fall
    step(own_rise, None, column, half)
    far_rise = far_fall = far
    for t in range(1, half):
        far_rise, far_fall = step(far_rise, far_fall, 1 - column, t)
    step(None, far_fall, 1 - column, half)
    info = jnp.stack([me] + index).astype(jnp.int32)

    vmem = pl.BlockSpec(memory_space=pltpu.VMEM)
    rows, gates = pl.pallas_call(
        functools.partial(expert_kernel, blocks, tok, top, cap),
        in_specs=[pl.BlockSpec(memory_space=pltpu.SMEM)] + [vmem] * blocks,
        out_specs=[vmem, vmem],
        out_shape=[
            jax.ShapeDtypeStruct((2 * slots, width), bf16),
            jax.ShapeDtypeStruct((8, 2 * slots), f32),
        ],
        scratch_shapes=[
            pltpu.VMEM((2, slots, width), f32),
            pltpu.VMEM((2, slots, 128), f32),
            pltpu.VMEM((blocks * META, top * tok), f32),
        ],
        compiler_params=pltpu.CompilerParams(vmem_limit_bytes=32 * 1024 * 1024),
        cost_estimate=pl.CostEstimate(
            flops=ff * width * slots, bytes_accessed=8 * 1024 * 1024, transcendentals=0
        ),
    )(info, *msgs)
    partial = lax.dot_general(
        down_weight.reshape(ff, width), rows, NT, preferred_element_type=f32
    ).astype(bf16)

    terms = lax.psum_scatter(partial, "dp", scatter_dimension=0, tiled=True)
    slot_grad = lax.psum(
        jnp.sum(partial.astype(f32) * saved_all.astype(f32), axis=0), "dp"
    )
    home = jnp.transpose(slot_grad.reshape(2, blocks, cap), (1, 0, 2)).reshape(blocks, 2 * cap)
    back = lax.all_to_all(home, "expert", split_axis=0, concat_axis=0, tiled=True)
    logits = pl.pallas_call(
        functools.partial(logits_kernel, cap),
        out_shape=[jax.ShapeDtypeStruct((top, tok), f32)] * 2,
        scratch_shapes=[pltpu.VMEM((top, tok), f32)],
    )(*side, back)
    hidden = []
    for m in range(2):
        cols = slice(m * slots, (m + 1) * slots)
        scaled = (gates[:1, cols] * terms[:, cols].astype(f32)).astype(bf16)
        hidden.append(scaled.reshape(1, ff_shard, 1, slots))
    return (*hidden, *(g.T[None] for g in logits))


def solution(mesh):
    in_specs = (
        P("section", "expert", "dp"),
        P("section", "expert", "dp"),
        P("section", "expert", None),
        P("section", "expert", None),
        P("section", "expert", None),
        P("section", "expert", None),
        P("section", "expert", None, "dp"),
        P("section", "dp", "expert", None),
        P("section", "dp", "expert", None),
    )
    out_specs = (
        P("section", "dp", "expert", None),
        P("section", "dp", "expert", None),
        P("section", "expert", None),
        P("section", "expert", None),
    )
    return jax.shard_map(shards, mesh=mesh, in_specs=in_specs, out_specs=out_specs, check_vma=False)
```

```python
import functools

import jax
import jax.numpy as jnp
from jax import lax
from jax.experimental import pallas as pl
from jax.experimental.pallas import tpu as pltpu
from jax.sharding import PartitionSpec as P

route_scale = 2.5
META = 8
NT = (((1,), (1,)), ((), ()))
f32 = jnp.float32
bf16 = jnp.bfloat16


def pack_kernel(rf, sf, rr, sr, out, buf):
    top, tok = rf.shape
    buf[...] = jnp.zeros_like(buf)
    for m, (routes, scores) in enumerate(((rf, sf), (rr, sr))):
        ids = routes[...].astype(f32)
        s = scores[...]
        gate = route_scale * s / jnp.sum(s, axis=0, keepdims=True)
        for k in range(top):
            buf[2 * m : 2 * m + 1, k * tok : (k + 1) * tok] = ids[k : k + 1]
            buf[2 * m + 1 : 2 * m + 2, k * tok : (k + 1) * tok] = gate[k : k + 1]
    out[...] = buf[...].astype(out.dtype)


def expert_kernel(blocks, tok, top, cap, info, *refs):
    msgs = refs[:blocks]
    w_hbm, saved_hbm, part_hbm, slot_ref, gate_ref = refs[blocks : blocks + 5]
    rows, rows16, gcol, meta, w_ref, saved_ref, part_ref, w_sem, saved_sem, part_sem = refs[blocks + 5 :]
    slots = blocks * cap
    lanes = 2 * tok
    tiles = w_sem.shape[0]
    tile = w_ref.shape[0] // tiles
    parts = [pl.ds(i * tile, tile) for i in range(tiles)]
    fetched = []
    for i, at in enumerate(parts):
        pair = (
            pltpu.make_async_copy(w_hbm.at[at], w_ref.at[at], w_sem.at[i]),
            pltpu.make_async_copy(saved_hbm.at[at], saved_ref.at[at], saved_sem.at[i]),
        )
        for copy in pair:
            copy.start()
        fetched.append(pair)

    for b in range(blocks):
        meta[b * META : (b + 1) * META, :] = msgs[b][lanes : lanes + META, : top * tok].astype(f32)
    vals = meta[...]
    mine = (vals == info[0].astype(f32)).astype(f32)
    t_in = lax.rem(lax.broadcasted_iota(jnp.int32, (top * tok, lanes), 0), tok)
    t_out = lax.rem(lax.broadcasted_iota(jnp.int32, (top * tok, lanes), 1), tok)
    same = (t_in == t_out).astype(f32).astype(bf16)
    before = (t_in < t_out).astype(f32).astype(bf16)
    hot = mine.astype(bf16)
    named = jnp.dot(hot, same, preferred_element_type=f32)
    place = jnp.dot(hot, before, preferred_element_type=f32)
    picked = (pltpu.roll(mine, 1, 0) * vals).astype(bf16)
    gates = jnp.dot(picked, same, preferred_element_type=f32)
    rising = lax.broadcasted_iota(jnp.int32, (1, lanes), 1) >= tok
    shift = jnp.where(rising, float(cap), 0.0)
    slot_id = lax.broadcasted_iota(jnp.int32, (2 * cap, lanes), 0).astype(f32)
    for b in range(blocks):
        r = b * META
        name = jnp.where(rising, named[r + 2 : r + 3], named[r : r + 1])
        pos = jnp.where(rising, place[r + 2 : r + 3], place[r : r + 1])
        gate = jnp.where(rising, gates[r + 3 : r + 4], gates[r + 1 : r + 2])
        target = jnp.where(name > 0.5, pos + shift, -1.0)
        put = (slot_id == target).astype(f32)
        got = jnp.dot(put.astype(bf16), msgs[b][:lanes, :], preferred_element_type=f32)
        col = jnp.broadcast_to(jnp.sum(put * gate, axis=1, keepdims=True), (2 * cap, gcol.shape[2]))
        at = pl.ds(pl.multiple_of(info[1 + b] * cap, 8), cap)
        for m in range(2):
            rows[m, at, :] = got[m * cap : (m + 1) * cap]
            gcol[m, at, :] = col[m * cap : (m + 1) * cap]
    first = (lax.broadcasted_iota(jnp.int32, (8, gcol.shape[2]), 1) == 0).astype(f32).astype(bf16)
    for m in range(2):
        rows16[m * slots : (m + 1) * slots, :] = rows[m].astype(bf16)
        gate_ref[:, m * slots : (m + 1) * slots] = lax.dot_general(
            first, gcol[m].astype(bf16), NT, preferred_element_type=f32
        )

    sent = []
    for i, at in enumerate(parts):
        for copy in fetched[i]:
            copy.wait()
        part = lax.dot_general(w_ref[at, :], rows16[...], NT, preferred_element_type=f32).astype(bf16)
        part_ref[at, :] = part
        prod = part.astype(f32) * saved_ref[at, :].astype(f32)
        total = jnp.sum(prod.reshape(-1, 8, 2 * slots), axis=0)
        slot_ref[...] = total if i == 0 else slot_ref[...] + total
        copy = pltpu.make_async_copy(part_ref.at[at], part_hbm.at[at], part_sem.at[i])
        copy.start()
        sent.append(copy)
    for copy in sent:
        copy.wait()


def logits_kernel(cap, rf, sf, rr, sr, back, out_f, out_r, grad):
    top, tok = rf.shape
    experts = back.shape[0]
    ids = lax.broadcasted_iota(jnp.int32, (experts, tok), 0)
    t0 = lax.broadcasted_iota(jnp.int32, (tok, tok), 0)
    t1 = lax.broadcasted_iota(jnp.int32, (tok, tok), 1)
    before = (t0 < t1).astype(f32).astype(bf16)
    for m, (routes, scores, out) in enumerate(((rf, sf, out_f), (rr, sr, out_r))):
        named = jnp.zeros((experts, tok), f32)
        for k in range(top):
            named += (routes[k : k + 1, :] == ids).astype(f32)
        place = jnp.dot(named.astype(bf16), before, preferred_element_type=f32)
        vals = jnp.zeros((experts, tok), f32)
        for c in range(cap):
            vals += jnp.where(place == float(c), back[:, m * cap + c : m * cap + c + 1], 0.0)
        for k in range(top):
            chosen = jnp.where(routes[k : k + 1, :] == ids, vals, 0.0)
            grad[k : k + 1, :] = jnp.sum(chosen, axis=0, keepdims=True)
        s = scores[...]
        total = jnp.sum(s, axis=0, keepdims=True)
        mean = jnp.sum(grad[...] * s, axis=0, keepdims=True) / total
        out[...] = route_scale / total * (grad[...] - mean) * s * (1.0 - s)


def shards(
    falling_grad,
    rising_grad,
    routes_falling,
    routes_rising,
    scores_falling,
    scores_rising,
    down_weight,
    saved_falling,
    saved_rising,
):
    blocks = lax.axis_size("expert")
    sections = lax.axis_size("section")
    dp = lax.axis_size("dp")
    tok, width = falling_grad.shape[1:]
    top = routes_falling.shape[2]
    ff_shard, slots = saved_falling.shape[1], saved_falling.shape[3]
    cap = slots // blocks
    ff = ff_shard * dp
    depth = blocks // 2
    lanes = 2 * tok

    side = (
        routes_falling[0].T,
        scores_falling[0].T,
        routes_rising[0].T,
        scores_rising[0].T,
    )
    def hop(array, by, flip):
        pairs = [
            (s * blocks + e, (s + by) % sections * blocks + (e ^ flip))
            for s in range(sections)
            for e in range(blocks)
        ]
        return lax.ppermute(array, ("section", "expert"), pairs)

    own_f, own_r = hop(falling_grad[0], -1, 0), hop(rising_grad[0], 1, 0)
    meta = pl.pallas_call(
        pack_kernel,
        out_shape=jax.ShapeDtypeStruct((META, width), bf16),
        scratch_shapes=[pltpu.VMEM((META, width), f32)],
    )(*side)
    own = jnp.concatenate([own_f, own_r, meta], axis=0)
    far = hop(own, 0, 1)

    saved = jnp.concatenate(
        [saved_falling.reshape(ff_shard, slots), saved_rising.reshape(ff_shard, slots)], axis=1
    )
    own_ring, saved = lax.optimization_barrier((own, saved))
    saved_all = lax.all_gather(saved, "dp", tiled=True)

    up = [(i, (i + 2) % blocks) for i in range(blocks)]
    down = [(i, (i - 2) % blocks) for i in range(blocks)]
    me = lax.axis_index("expert")
    level, column = me // 2, me % 2
    msgs, index = [own, far], [me, level * 2 + 1 - column]

    def step(rise, fall, side, t):
        if rise is not None:
            rise = lax.ppermute(rise, "expert", up)
            msgs.append(rise)
            index.append((level - t) % depth * 2 + side)
        if fall is not None:
            fall = lax.ppermute(fall, "expert", down)
            msgs.append(fall)
            index.append((level + t) % depth * 2 + side)
        return rise, fall

    half = depth // 2
    own_rise = own_fall = own_ring
    for t in range(1, half):
        own_rise, own_fall = step(own_rise, own_fall, column, t)
        if t == 1:
            own_rise, own_fall, far = lax.optimization_barrier((own_rise, own_fall, far))
            msgs[1:] = far, own_rise, own_fall
        if t <= 2:
            far_fall = hop(own_fall, 0, 1)
            msgs.append(far_fall)
            index.append((level + t) % depth * 2 + 1 - column)
    step(None, own_fall, column, half)
    far_rise = far
    for t in range(1, half):
        far_rise, _ = step(far_rise, None, 1 - column, t)
    for t in range(3, half + 1):
        _, far_fall = step(None, far_fall, 1 - column, t)
    info = jnp.stack([me] + index).astype(jnp.int32)

    tiles = max(1, ff // 256)
    vmem, hbm = pl.BlockSpec(memory_space=pltpu.VMEM), pl.BlockSpec(memory_space=pltpu.HBM)
    partial, slot_part, gates = pl.pallas_call(
        functools.partial(expert_kernel, blocks, tok, top, cap),
        in_specs=[pl.BlockSpec(memory_space=pltpu.SMEM)] + [vmem] * blocks + [hbm, hbm],
        out_specs=[hbm, vmem, vmem],
        out_shape=[
            jax.ShapeDtypeStruct((ff, 2 * slots), bf16),
            jax.ShapeDtypeStruct((8, 2 * slots), f32),
            jax.ShapeDtypeStruct((8, 2 * slots), f32),
        ],
        scratch_shapes=[
            pltpu.VMEM((2, slots, width), f32),
            pltpu.VMEM((2 * slots, width), bf16),
            pltpu.VMEM((2, slots, 128), f32),
            pltpu.VMEM((blocks * META, top * tok), f32),
            pltpu.VMEM((ff, width), bf16),
            pltpu.VMEM((ff, 2 * slots), bf16),
            pltpu.VMEM((ff, 2 * slots), bf16),
            pltpu.SemaphoreType.DMA((tiles,)),
            pltpu.SemaphoreType.DMA((tiles,)),
            pltpu.SemaphoreType.DMA((tiles,)),
        ],
        compiler_params=pltpu.CompilerParams(vmem_limit_bytes=50 * 1024 * 1024),
        cost_estimate=pl.CostEstimate(
            flops=4 * ff * width * slots, bytes_accessed=16 * 1024 * 1024, transcendentals=0
        ),
    )(info, *msgs, down_weight.reshape(ff, width), saved_all)

    terms = lax.psum_scatter(partial, "dp", scatter_dimension=0, tiled=True)
    slot_grad = lax.psum(jnp.sum(slot_part, axis=0), "dp")
    home = jnp.transpose(slot_grad.reshape(2, blocks, cap), (1, 0, 2)).reshape(blocks, 2 * cap)
    back = lax.all_to_all(home, "expert", split_axis=0, concat_axis=0, tiled=True)
    logits = pl.pallas_call(
        functools.partial(logits_kernel, cap),
        out_shape=[jax.ShapeDtypeStruct((top, tok), f32)] * 2,
        scratch_shapes=[pltpu.VMEM((top, tok), f32)],
    )(*side, back)
    hidden = []
    for m in range(2):
        cols = slice(m * slots, (m + 1) * slots)
        scaled = (gates[:1, cols] * terms[:, cols].astype(f32)).astype(bf16)
        hidden.append(scaled.reshape(1, ff_shard, 1, slots))
    return (*hidden, *(g.T[None] for g in logits))


def solution(mesh):
    in_specs = (
        P("section", "expert", "dp"),
        P("section", "expert", "dp"),
        P("section", "expert", None),
        P("section", "expert", None),
        P("section", "expert", None),
        P("section", "expert", None),
        P("section", "expert", None, "dp"),
        P("section", "dp", "expert", None),
        P("section", "dp", "expert", None),
    )
    out_specs = (
        P("section", "dp", "expert", None),
        P("section", "dp", "expert", None),
        P("section", "expert", None),
        P("section", "expert", None),
    )
    return jax.shard_map(shards, mesh=mesh, in_specs=in_specs, out_specs=out_specs, check_vma=False)
```
